512 devices in a mesh: px: 32 (over z, x), py: 16 (over y, core).
Axes of the slice: x: 4, y: 8, z: 8, core: 2. Of those that a mesh axis runs over, the one named last changes fastest.
Arguments:
- node_latents: bfloat16 [32, 16, 2048, 128], P('px', 'py'), may hold values from -6 to 6
- edge_latents: bfloat16 [32, 16, 1024, 128], P('px', 'py'), may hold values from -6 to 6
- edge_senders: int32 [32, 16, 1024], P('px', 'py'), may hold values from 0 to 3071
- edge_receivers: int32 [32, 16, 1024], P('px', 'py'), may hold values from 0 to 2047
- send_rows: int32 [32, 16, 256], P('px', 'py'), may hold values from 0 to 2047
- clusters: int32 [32, 16, 2048], P('px', 'py'), may hold values from 0 to 4095, as said below
- coarse_senders: int32 [32, 16, 1024], P('px', 'py'), may hold values from 0 to 1279
- coarse_receivers: int32 [32, 16, 1024], P('px', 'py'), may hold values from 0 to 255
- fine_edge_in: bfloat16 [384, 128], replicated, may hold values from -0.3125 to 0.3125
- fine_edge_out: bfloat16 [128, 128], replicated, may hold values from -0.5 to 0.5
- fine_node_in: bfloat16 [256, 128], replicated, may hold values from -0.375 to 0.375
- fine_node_out: bfloat16 [128, 128], replicated, may hold values from -0.5 to 0.5
- coarse_edge_in: bfloat16 [256, 128], replicated, may hold values from -0.375 to 0.375
- coarse_edge_out: bfloat16 [128, 128], replicated, may hold values from -0.5 to 0.5
- coarse_node_in: bfloat16 [256, 128], replicated, may hold values from -0.375 to 0.375
- coarse_node_out: bfloat16 [128, 128], replicated, may hold values from -0.5 to 0.5
- prolong_in: bfloat16 [256, 128], replicated, may hold values from -0.375 to 0.375
- prolong_out: bfloat16 [128, 128], replicated, may hold values from -0.5 to 0.5
Outputs:
- node_out: bfloat16 [32, 16, 2048, 128], P('px', 'py')
- edge_out: bfloat16 [32, 16, 1024, 128], P('px', 'py')
The draws below stay inside these ranges and needn't reach their ends.
Inputs may be any that keep to these rules, and one draw needn't show every extreme that they name: `clusters`: A cell of partition (i, j) belongs to a cluster of partition (i, j-1), (i, j) or (i, j+1) of the same row.
All inputs are finite; a program needn't handle non-finite values.
Results may differ from the reference program's by a relative error of at most 0.0095.
Values may be sent and summed in bfloat16 or wider, within the bound.
No kernel may reach another device: no remote copies, remote signals or barrier semaphores. Data moves between devices by JAX's collectives and lax.ppermute only.
A program may use at most 64 MiB of HBM per device.

```python
from functools import partial
import jax
import jax.numpy as jnp
from jax import lax

LATENT = 128
CELL_DEV = 2048
EDGE_DEV = 1024
RIM_DEV = 256
CLUS_DEV = 256
CEDGE_DEV = 1024
CLUS_ROW = 4096
FAN = 8
GRID_X = 32
GRID_Y = 16


def draw_clusters(key, part):
    key = jax.random.fold_in(key, 11)
    local_key, side_key = jax.random.split(key)
    shape = (GRID_X, GRID_Y, CELL_DEV)
    local = jax.random.randint(local_key, shape, 0, CLUS_DEV)
    side = jax.random.randint(side_key, shape, 0, 20)
    offset = jnp.where(side == 0, -1, jnp.where(side == 19, 1, 0))
    column = jnp.arange(GRID_Y, dtype=jnp.int32)[None, :, None]
    target = column + offset
    offset = jnp.where((target < 0) | (target >= GRID_Y), 0, offset)
    position = jnp.arange(CELL_DEV, dtype=jnp.int32)[None, None, :]
    local = jnp.where(position == 0, CLUS_DEV - 1, jnp.where(position == 1, 0, local))
    offset = jnp.where(position < 2, 0, offset)
    return ((column + offset) * CLUS_DEV + local).astype(jnp.int32)


def draw_coarse_senders(key, part):
    key = jax.random.fold_in(key, 23)
    block_key, row_key = jax.random.split(key)
    shape = (GRID_X, GRID_Y, CEDGE_DEV)
    pick = jax.random.randint(block_key, shape, 0, 8)
    block = jnp.where(pick < 4, pick + 1, 0)
    local = jax.random.randint(row_key, shape, 0, CLUS_DEV)
    value = block * CLUS_DEV + local
    position = jnp.arange(CEDGE_DEV, dtype=jnp.int32)[None, None, :]
    value = jnp.where(position == 0, 5 * CLUS_DEV - 1, jnp.where(position == 1, 0, value))
    return value.astype(jnp.int32)


def with_ends(result, own_key, low, top_value):
    longest = result.shape.index(max(result.shape))
    spots = []
    for shift in (0, 1):
        where = [jax.random.randint(jax.random.fold_in(own_key, axis), (), 0, length) for axis, length in enumerate(result.shape)]
        where[longest] = (where[longest] + shift) % result.shape[longest]
        spots.append(tuple(where))
    return result.at[spots[0]].set(low).at[spots[1]].set(top_value)


def steps_of(own_key, extent, cuts, smallest, largest):
    level = 1.0
    for axis_at, shards_of in cuts:
        steps = jax.random.uniform(jax.random.fold_in(jax.random.fold_in(own_key, 6), axis_at), (shards_of,), jnp.float32, smallest / len(cuts), largest / len(cuts))
        level = level * jnp.repeat(jnp.exp(steps), extent[axis_at] // shards_of).reshape((-1,) + (1,) * (len(extent) - 1 - axis_at))
    return level


def normal_values(stream_key, shape, deviation, limit, pieces=(), held_as=jnp.bfloat16):
    loudness = steps_of(stream_key, shape, pieces, -0.22, 0.18) if pieces else 1.0
    entries = jax.random.normal(stream_key, shape, jnp.float32) * deviation * loudness
    return jnp.minimum(jnp.maximum(entries, -limit), limit).astype(held_as)


def setup_inputs(seed: int = 0) -> dict:
    keys = jax.random.split(jax.random.key(seed), 19)
    node_latents = normal_values(keys[0], (GRID_X, GRID_Y, CELL_DEV, LATENT), 1.0, 6.0, ((0, 32), (1, 16)))
    edge_latents = normal_values(keys[1], (GRID_X, GRID_Y, EDGE_DEV, LATENT), 1.0, 6.0, ((0, 32), (1, 16)))
    edge_senders = with_ends(jax.random.randint(keys[2], (GRID_X, GRID_Y, EDGE_DEV), 0, CELL_DEV + 4 * RIM_DEV), jax.random.fold_in(keys[2], 1), 0, (CELL_DEV + 4 * RIM_DEV) - 1).astype(jnp.int32)
    edge_receivers = with_ends(jax.random.randint(keys[3], (GRID_X, GRID_Y, EDGE_DEV), 0, CELL_DEV), jax.random.fold_in(keys[3], 1), 0, CELL_DEV - 1).astype(jnp.int32)
    send_rows = with_ends(jax.random.randint(keys[4], (GRID_X, GRID_Y, RIM_DEV), 0, CELL_DEV), jax.random.fold_in(keys[4], 1), 0, CELL_DEV - 1).astype(jnp.int32)
    clusters = draw_clusters(jax.random.fold_in(keys[18], 71), 0)
    coarse_senders = draw_coarse_senders(jax.random.fold_in(keys[18], 71), 0)
    coarse_receivers = with_ends(jax.random.randint(keys[7], (GRID_X, GRID_Y, CEDGE_DEV), 0, CLUS_DEV), jax.random.fold_in(keys[7], 1), 0, CLUS_DEV - 1).astype(jnp.int32)
    fine_edge_in = normal_values(keys[8], (3 * LATENT, LATENT), (3 * LATENT) ** -0.5, 0.3125)
    fine_edge_out = normal_values(keys[9], (LATENT, LATENT), LATENT ** -0.5, 0.5)
    fine_node_in = normal_values(keys[10], (2 * LATENT, LATENT), (2 * LATENT) ** -0.5, 0.375)
    fine_node_out = normal_values(keys[11], (LATENT, LATENT), LATENT ** -0.5, 0.5)
    coarse_edge_in = normal_values(keys[12], (2 * LATENT, LATENT), (2 * LATENT) ** -0.5, 0.375)
    coarse_edge_out = normal_values(keys[13], (LATENT, LATENT), LATENT ** -0.5, 0.5)
    coarse_node_in = normal_values(keys[14], (2 * LATENT, LATENT), (2 * LATENT) ** -0.5, 0.375)
    coarse_node_out = normal_values(keys[15], (LATENT, LATENT), LATENT ** -0.5, 0.5)
    prolong_in = normal_values(keys[16], (2 * LATENT, LATENT), (2 * LATENT) ** -0.5, 0.375)
    prolong_out = normal_values(keys[17], (LATENT, LATENT), LATENT ** -0.5, 0.5)
    return {"node_latents": node_latents, "edge_latents": edge_latents, "edge_senders": edge_senders, "edge_receivers": edge_receivers, "send_rows": send_rows, "clusters": clusters, "coarse_senders": coarse_senders, "coarse_receivers": coarse_receivers, "fine_edge_in": fine_edge_in, "fine_edge_out": fine_edge_out, "fine_node_in": fine_node_in, "fine_node_out": fine_node_out, "coarse_edge_in": coarse_edge_in, "coarse_edge_out": coarse_edge_out, "coarse_node_in": coarse_node_in, "coarse_node_out": coarse_node_out, "prolong_in": prolong_in, "prolong_out": prolong_out}


def layer_norm(values):
    mean = lax.optimization_barrier(jnp.mean(values, axis=-1, keepdims=True))
    centred = values - mean
    spread = lax.optimization_barrier(jnp.mean(centred * centred, axis=-1, keepdims=True))
    return centred * lax.rsqrt(spread + 1e-05)

def perceptron(inputs, first, second):
    hidden = jnp.maximum(jnp.dot(inputs, first, preferred_element_type=jnp.float32), 0.0).astype(jnp.bfloat16)
    return layer_norm(jnp.dot(hidden, second, preferred_element_type=jnp.float32))

def neighbour_tables(blocks):
    padded = jnp.pad(blocks, ((1, 1), (1, 1), (0, 0), (0, 0)))
    return jnp.concatenate([blocks, padded[:-2, 1:-1], padded[2:, 1:-1], padded[1:-1, :-2], padded[1:-1, 2:]], axis=2)

def fine_block(nodes, edges, table, senders, receivers, weights):
    edge_in, edge_out, node_in, node_out = weights
    inputs = jnp.concatenate([edges, jnp.take(table, senders, axis=0), jnp.take(nodes, receivers, axis=0)], axis=1)
    message = perceptron(inputs, edge_in, edge_out)
    new_edges = (edges.astype(jnp.float32) + message).astype(jnp.bfloat16)
    gathered = jax.ops.segment_sum(message, receivers, num_segments=nodes.shape[0]).astype(jnp.bfloat16)
    update = perceptron(jnp.concatenate([nodes, gathered], axis=1), node_in, node_out)
    new_nodes = (nodes.astype(jnp.float32) + update).astype(jnp.bfloat16)
    return (new_nodes, new_edges)

def fine_layer(nodes, edges, senders, receivers, send_rows, weights):
    outgoing = jnp.take_along_axis(nodes, send_rows[..., None], axis=2)
    padded = jnp.pad(outgoing, ((1, 1), (1, 1), (0, 0), (0, 0)))
    tables = jnp.concatenate([nodes, padded[:-2, 1:-1], padded[2:, 1:-1], padded[1:-1, :-2], padded[1:-1, 2:]], axis=2)

    def one_row(items):
        return jax.vmap(partial(fine_block, weights=weights))(*items)
    return lax.map(one_row, (nodes, edges, tables, senders, receivers))

def reference(node_latents, edge_latents, edge_senders, edge_receivers, send_rows, clusters, coarse_senders, coarse_receivers, fine_edge_in, fine_edge_out, fine_node_in, fine_node_out, coarse_edge_in, coarse_edge_out, coarse_node_in, coarse_node_out, prolong_in, prolong_out):
    weights = (fine_edge_in, fine_edge_out, fine_node_in, fine_node_out)
    cells_one, edges_one = fine_layer(node_latents, edge_latents, edge_senders, edge_receivers, send_rows, weights)

    def pool_row(items):
        rows, labels = items
        return jax.ops.segment_sum(rows.reshape(-1, LATENT).astype(jnp.float32), labels.reshape(-1), num_segments=CLUS_ROW)
    sums = lax.map(pool_row, (cells_one, clusters))
    pooled = (sums / FAN).astype(jnp.bfloat16)
    pooled_blocks = pooled.reshape(GRID_X, GRID_Y, CLUS_DEV, LATENT)
    coarse_tables = neighbour_tables(pooled_blocks)

    def coarse_block(own, table, senders, receivers):
        inputs = jnp.concatenate([jnp.take(table, senders, axis=0), jnp.take(own, receivers, axis=0)], axis=1)
        message = perceptron(inputs, coarse_edge_in, coarse_edge_out)
        gathered = jax.ops.segment_sum(message, receivers, num_segments=CLUS_DEV).astype(jnp.bfloat16)
        update = perceptron(jnp.concatenate([own, gathered], axis=1), coarse_node_in, coarse_node_out)
        return (own.astype(jnp.float32) + update).astype(jnp.bfloat16)

    def coarse_row(items):
        return jax.vmap(coarse_block)(*items)
    coarse = lax.map(coarse_row, (pooled_blocks, coarse_tables, coarse_senders, coarse_receivers))
    coarse = coarse.reshape(GRID_X, CLUS_ROW, LATENT)

    def prolong_row(items):
        rows, labels, level = items

        def one_block(cells, cell_labels):
            looked = jnp.take(level, cell_labels, axis=0)
            update = perceptron(jnp.concatenate([cells, looked], axis=1), prolong_in, prolong_out)
            return (cells.astype(jnp.float32) + update).astype(jnp.bfloat16)
        return jax.vmap(one_block)(rows, labels)
    cells_two = lax.map(prolong_row, (cells_one, clusters, coarse))
    node_out, edge_out = fine_layer(cells_two, edges_one, edge_senders, edge_receivers, send_rows, weights)
    return (node_out, edge_out)
```

```python
import functools

import jax
import jax.numpy as jnp
from jax import lax
from jax.experimental import pallas as pl
from jax.experimental.pallas import tpu as pltpu
from jax.sharding import PartitionSpec as P

LATENT = 128
CELLS = 2048
EDGES = 1024
RIM = 256
CLUS = 256
CEDGES = 1024
FAN = 8
ROWS = 4
BF16 = jnp.bfloat16
F32 = jnp.float32
VMEM = pl.BlockSpec(memory_space=pltpu.VMEM)
SMEM = pl.BlockSpec(memory_space=pltpu.SMEM)
PARAMS = pltpu.CompilerParams(vmem_limit_bytes=24 * 1024 * 1024)


def cost(flops, moved):
    return pl.CostEstimate(flops=flops, bytes_accessed=moved, transcendentals=0)


def dot(a, b):
    return jnp.dot(a, b, preferred_element_type=F32)


def column(ref, start, count):
    parts = []
    for k in range(count):
        row = ref[pl.ds(start + k, 1), :]
        parts.append(jnp.transpose(jnp.broadcast_to(row, (128, 128))))
    return jnp.concatenate(parts, axis=0)


def pick_rows(code, depth, low):
    code = code.astype(F32).astype(BF16)
    blocks = []
    for b in range(depth // 128):
        lane = lax.broadcasted_iota(jnp.int32, code.shape, 1) + (low + 128 * b)
        hit = code == lane.astype(F32).astype(BF16)
        blocks.append(jnp.where(hit, jnp.ones_like(code), jnp.zeros_like(code)))
    return jnp.concatenate(blocks, axis=1)


def pick_columns(ref, code_of, depth, low, count):
    row = lax.broadcasted_iota(jnp.int32, (depth, 128), 0) + low
    row = row.astype(F32).astype(BF16)
    blocks = []
    for c in range(count):
        code = code_of(ref[pl.ds(c, 1), :]).astype(F32).astype(BF16)
        hit = jnp.broadcast_to(code, (depth, 128)) == row
        blocks.append(jnp.where(hit, jnp.ones_like(row), jnp.zeros_like(row)))
    return jnp.concatenate(blocks, axis=1)


def side_by_side(table, folds):
    depth = table.shape[0] // folds
    return jnp.concatenate([table[f * depth : (f + 1) * depth] for f in range(folds)], axis=1)


def choose(wide, which, folds):
    out = wide[:, :LATENT]
    for f in range(1, folds):
        out = jnp.where(which == f, wide[:, f * LATENT : (f + 1) * LATENT], out)
    return out


def layer_norm(values):
    mean = jnp.mean(values, axis=-1, keepdims=True)
    centred = values - mean
    spread = jnp.mean(centred * centred, axis=-1, keepdims=True)
    return centred * lax.rsqrt(spread + 1e-05)


def finish(pre, second):
    return layer_norm(dot(jnp.maximum(pre, 0.0).astype(BF16), second))


def from_cells(table, index):
    code = jnp.where(index < CELLS, (index & 511) - 256, 512)
    wide = dot(pick_rows(code, 512, -256), table)
    return choose(wide, index >> 9, 4).astype(BF16)


def from_halo(table, index):
    code = jnp.where(index >= 0, index & 255, 512)
    wide = dot(pick_rows(code, 256, 0), table)
    return choose(wide, index >> 8, 4).astype(BF16)


def halo_table(flags, left, right, first, second, cross):
    a, b, c = first[...], second[...], cross[...]
    zero = jnp.zeros_like(a)
    up = jnp.where(flags[0] == 0, a, jnp.where(flags[0] == 1, b, jnp.where(flags[0] == 2, c, zero)))
    down = jnp.where(flags[1] == 0, a, jnp.where(flags[1] == 1, b, jnp.where(flags[1] == 2, c, zero)))
    west = jnp.where(flags[2] == 0, zero, left[...])
    east = jnp.where(flags[3] == 0, zero, right[...])
    return jnp.concatenate([up, down, west, east], axis=1)


def outgoing_kernel(nodes, rows, out):
    table = side_by_side(nodes[...], 4)
    out[...] = from_cells(table, column(rows, 0, 2))


def fine_local_kernel(nodes, edges, senders, receivers, first, out):
    table = side_by_side(nodes[...], 4)

    def body(i, carry):
        index = jnp.concatenate([column(senders, 2 * i, 2), column(receivers, 2 * i, 2)], axis=0)
        near = from_cells(table, index)
        at = pl.ds(pl.multiple_of(i * 256, 256), 256)
        inputs = jnp.concatenate([edges[at, :], near[:256], near[256:]], axis=1)
        out[at, :] = dot(inputs, first[...])
        return carry

    lax.fori_loop(0, 4, body, 0)


def fine_rest(
    flags, pre, edges, nodes, senders, receivers, halo, edge_in, edge_out, node_in, node_out, new_edges, wide, sums
):
    table = halo_table(flags, *halo)

    def edge_body(i, carry):
        at = pl.ds(pl.multiple_of(i * 256, 256), 256)
        far = from_halo(table, column(senders, 2 * i, 2) - CELLS)
        message = finish(pre[at, :] + dot(far, edge_in[LATENT : 2 * LATENT, :]), edge_out[...])
        new_edges[at, :] = (edges[at, :].astype(F32) + message).astype(BF16)
        quarter = column(receivers, 2 * i, 2) >> 9
        wide[at, :] = jnp.concatenate(
            [jnp.where(quarter == f, message, 0.0) for f in range(4)], axis=1
        ).astype(BF16)
        return carry

    lax.fori_loop(0, 4, edge_body, 0)
    spread = pick_columns(receivers, lambda r: (r & 511) - 256, 512, -256, 8)
    total = dot(spread, wide[...]).astype(BF16)
    for f in range(4):
        sums[f] = total[:, f * LATENT : (f + 1) * LATENT]


def node_update(f, nodes, sums, node_in, node_out):
    at = pl.ds(pl.multiple_of(f * 512, 512), 512)
    cells = nodes[at, :]
    inputs = jnp.concatenate([cells, sums[f]], axis=1)
    return at, (cells.astype(F32) + finish(dot(inputs, node_in[...]), node_out[...])).astype(BF16)


def fine_pool_kernel(
    flags, pre, edges, nodes, senders, receivers, left, right, first, second, cross,
    edge_in, edge_out, node_in, node_out, labels,
    new_nodes, new_edges, own, to_left, to_right, wide, sums, masked,
):
    fine_rest(
        flags, pre, edges, nodes, senders, receivers, (left, right, first, second, cross),
        edge_in, edge_out, node_in, node_out, new_edges, wide, sums,
    )
    base = flags[4]

    def node_body(f, carry):
        at, cells = node_update(f, nodes, sums, node_in, node_out)
        new_nodes[at, :] = cells
        block = (column(labels, 4 * f, 4) - base) >> 8
        masked[at, :] = jnp.concatenate(
            [jnp.where(block == b, cells.astype(F32), 0.0) for b in range(3)], axis=1
        ).astype(BF16)
        return carry

    lax.fori_loop(0, 4, node_body, 0)
    spread = pick_columns(labels, lambda r: r & 255, 256, 0, 16)
    total = dot(spread, masked[...])
    to_left[...] = total[:, :LATENT].astype(BF16)
    own[...] = total[:, LATENT : 2 * LATENT]
    to_right[...] = total[:, 2 * LATENT :].astype(BF16)


def fine_last_kernel(
    flags, pre, edges, nodes, senders, receivers, left, right, first, second, cross,
    edge_in, edge_out, node_in, node_out,
    new_nodes, new_edges, wide, sums,
):
    fine_rest(
        flags, pre, edges, nodes, senders, receivers, (left, right, first, second, cross),
        edge_in, edge_out, node_in, node_out, new_edges, wide, sums,
    )

    def node_body(f, carry):
        at, cells = node_update(f, nodes, sums, node_in, node_out)
        new_nodes[at, :] = cells
        return carry

    lax.fori_loop(0, 4, node_body, 0)


def coarse_local_kernel(pooled, senders, receivers, first, out):
    table = pooled[...]

    def body(i, carry):
        index = jnp.concatenate([column(senders, 2 * i, 2), column(receivers, 2 * i, 2)], axis=0)
        code = jnp.where(index < CLUS, index, 512)
        near = dot(pick_rows(code, 256, 0), table).astype(BF16)
        at = pl.ds(pl.multiple_of(i * 256, 256), 256)
        out[at, :] = dot(jnp.concatenate([near[:256], near[256:]], axis=1), first[...])
        return carry

    lax.fori_loop(0, 4, body, 0)


def coarse_kernel(
    flags, pre, pooled, senders, receivers, left, right, first, second, cross,
    edge_in, edge_out, node_in, node_out, out, messages,
):
    table = halo_table(flags, left, right, first, second, cross)

    def body(i, carry):
        at = pl.ds(pl.multiple_of(i * 256, 256), 256)
        far = from_halo(table, column(senders, 2 * i, 2) - CLUS)
        message = finish(pre[at, :] + dot(far, edge_in[:LATENT, :]), edge_out[...])
        messages[at, :] = message.astype(BF16)
        return carry

    lax.fori_loop(0, 4, body, 0)
    spread = pick_columns(receivers, lambda r: r, 256, 0, 8)
    gathered = dot(spread, messages[...]).astype(BF16)
    own = pooled[...]
    update = finish(dot(jnp.concatenate([own, gathered], axis=1), node_in[...]), node_out[...])
    out[...] = (own.astype(F32) + update).astype(BF16)


def prolong_kernel(flags, cells, labels, own, left, right, rows, first, second, new_cells, outgoing):
    table = jnp.concatenate([left[...], own[...], right[...]], axis=1)
    base = flags[4]

    def body(f, carry):
        at = pl.ds(pl.multiple_of(f * 512, 512), 512)
        index = column(labels, 4 * f, 4) - base
        wide = dot(pick_rows(index & 255, 256, 0), table)
        looked = choose(wide, index >> 8, 3).astype(BF16)
        old = cells[at, :]
        update = finish(dot(jnp.concatenate([old, looked], axis=1), first[...]), second[...])
        new_cells[at, :] = (old.astype(F32) + update).astype(BF16)
        return carry

    lax.fori_loop(0, 4, body, 0)
    outgoing[...] = from_cells(side_by_side(new_cells[...], 4), column(rows, 0, 2))


def shape(*dims, dtype=BF16):
    return jax.ShapeDtypeStruct(dims, dtype)


def call(kernel, outs, ins, args, name, estimate, scratch=()):
    return pl.pallas_call(
        kernel,
        out_shape=outs,
        in_specs=ins,
        out_specs=jax.tree.map(lambda _: VMEM, outs),
        scratch_shapes=scratch,
        compiler_params=PARAMS,
        cost_estimate=estimate,
        name=name,
    )(*args)


def snake(count_x, count_y):
    pairs = []
    for i in range(count_x):
        for j in range(count_y):
            if j % 2 == 0:
                to = (i + 1, j) if i % ROWS < ROWS - 1 else (i, j + 1)
            else:
                to = (i - 1, j) if i % ROWS > 0 else (i, j - 1)
            pairs.append((i * count_y + j, to[0] * count_y + to[1]))
    return pairs


def exchange(block):
    count_x, count_y = lax.axis_size("px"), lax.axis_size("py")
    ring = snake(count_x, count_y)
    crossing = []
    for k in range(ROWS - 1, count_x - 1, ROWS):
        crossing += [(k, k + 1), (k + 1, k)]
    left, right = exchange_row(block, block)
    first = lax.ppermute(block, ("px", "py"), ring)
    second = lax.ppermute(block, ("px", "py"), [(b, a) for a, b in ring])
    cross = lax.ppermute(block, "px", crossing)
    return left, right, first, second, cross


def exchange_row(to_left, to_right):
    count = lax.axis_size("py")
    from_left = lax.ppermute(to_right, "py", [(i, (i + 1) % count) for i in range(count)])
    from_right = lax.ppermute(to_left, "py", [((i + 1) % count, i) for i in range(count)])
    return from_left, from_right


def on_device(
    node_latents, edge_latents, edge_senders, edge_receivers, send_rows, clusters, coarse_senders, coarse_receivers,
    fine_edge_in, fine_edge_out, fine_node_in, fine_node_out,
    coarse_edge_in, coarse_edge_out, coarse_node_in, coarse_node_out, prolong_in, prolong_out,
):
    nodes, edges = node_latents[0, 0], edge_latents[0, 0]
    senders, receivers = edge_senders.reshape(8, 128), edge_receivers.reshape(8, 128)
    rows, labels = send_rows.reshape(2, 128), clusters.reshape(16, 128)
    csenders, creceivers = coarse_senders.reshape(8, 128), coarse_receivers.reshape(8, 128)
    i, j = lax.axis_index("px"), lax.axis_index("py")
    last_i, last_j = lax.axis_size("px") - 1, lax.axis_size("py") - 1
    core, along = j % 2, i % ROWS
    up = jnp.where(along > 0, core, jnp.where(i > 0, 2, 3))
    down = jnp.where(along < ROWS - 1, 1 - core, jnp.where(i < last_i, 2, 3))
    flags = jnp.stack([up, down, j > 0, j < last_j, (j - 1) * CLUS]).astype(jnp.int32)

    def fine_local(nodes, edges):
        return call(
            fine_local_kernel, shape(EDGES, LATENT, dtype=F32), [VMEM] * 5,
            (nodes, edges, senders, receivers, fine_edge_in), "fine_local", cost(4_000_000_000, 2_000_000),
        )

    weights = (fine_edge_in, fine_edge_out, fine_node_in, fine_node_out)
    scratch = [pltpu.VMEM((EDGES, 512), BF16), pltpu.VMEM((4, 512, LATENT), BF16)]

    outgoing = call(outgoing_kernel, shape(RIM, LATENT), [VMEM] * 2, (nodes, rows), "outgoing", cost(10**9, 10**6))
    halo = exchange(outgoing)
    pre = fine_local(nodes, edges)
    cells, edges_one, own, to_left, to_right = call(
        fine_pool_kernel,
        [shape(CELLS, LATENT), shape(EDGES, LATENT), shape(CLUS, LATENT, dtype=F32)] + [shape(CLUS, LATENT)] * 2,
        [SMEM] + [VMEM] * 15,
        (flags, pre, edges, nodes, senders, receivers, *halo, *weights, labels),
        "fine_pool", cost(4_000_000_000, 2_000_000), scratch + [pltpu.VMEM((CELLS, 384), BF16)],
    )
    from_left, from_right = exchange_row(to_left, to_right)
    pooled = ((own + from_left + from_right) / FAN).astype(BF16)
    halo = exchange(pooled)
    pre = call(
        coarse_local_kernel, shape(CEDGES, LATENT, dtype=F32), [VMEM] * 4,
        (pooled, csenders, creceivers, coarse_edge_in), "coarse_local", cost(10**9, 10**6),
    )
    coarse = call(
        coarse_kernel, shape(CLUS, LATENT), [SMEM] + [VMEM] * 13,
        (flags, pre, pooled, csenders, creceivers, *halo,
         coarse_edge_in, coarse_edge_out, coarse_node_in, coarse_node_out),
        "coarse", cost(2 * 10**9, 10**6), [pltpu.VMEM((CEDGES, LATENT), BF16)],
    )
    left, right = exchange_row(coarse, coarse)
    cells_two, outgoing = call(
        prolong_kernel, [shape(CELLS, LATENT), shape(RIM, LATENT)], [SMEM] + [VMEM] * 8,
        (flags, cells, labels, coarse, left, right, rows, prolong_in, prolong_out),
        "prolong", cost(2 * 10**9, 10**6),
    )
    halo = exchange(outgoing)
    pre = fine_local(cells_two, edges_one)
    node_out, edge_out = call(
        fine_last_kernel, [shape(CELLS, LATENT), shape(EDGES, LATENT)], [SMEM] + [VMEM] * 14,
        (flags, pre, edges_one, cells_two, senders, receivers, *halo, *weights),
        "fine_last", cost(4_000_000_000, 2_000_000), scratch,
    )
    return node_out[None, None], edge_out[None, None]


def solution(mesh):
    split = P("px", "py", None)
    cells = P("px", "py", None, None)
    return jax.shard_map(
        on_device,
        mesh=mesh,
        in_specs=(cells, cells) + (split,) * 6 + (P(),) * 10,
        out_specs=(cells, cells),
        check_vma=False,
    )
```

```python
import functools

import jax
import jax.numpy as jnp
from jax import lax
from jax.experimental import pallas as pl
from jax.experimental.pallas import tpu as pltpu
from jax.sharding import PartitionSpec as P

LATENT = 128
CELLS = 2048
EDGES = 1024
RIM = 256
CLUS = 256
CEDGES = 1024
FAN = 8
ROWS = 4
CELL_PARTS = 2
BF16 = jnp.bfloat16
F32 = jnp.float32
VMEM = pl.BlockSpec(memory_space=pltpu.VMEM)
ANY = pl.BlockSpec(memory_space=pl.ANY)
SMEM = pl.BlockSpec(memory_space=pltpu.SMEM)
PARAMS = pltpu.CompilerParams(vmem_limit_bytes=24 * 1024 * 1024)


def cost(flops, moved):
    return pl.CostEstimate(flops=flops, bytes_accessed=moved, transcendentals=0)


def dot(a, b):
    return jnp.dot(a, b, preferred_element_type=F32)


def column(ref, start, count):
    parts = []
    for k in range(count):
        row = ref[pl.ds(start + k, 1), :]
        parts.append(jnp.transpose(jnp.broadcast_to(row, (128, 128))))
    return jnp.concatenate(parts, axis=0)


def pick_rows(code, depth, low):
    code = code.astype(F32).astype(BF16)
    blocks = []
    for b in range(depth // 128):
        lane = lax.broadcasted_iota(jnp.int32, code.shape, 1) + (low + 128 * b)
        hit = code == lane.astype(F32).astype(BF16)
        blocks.append(jnp.where(hit, jnp.ones_like(code), jnp.zeros_like(code)))
    return jnp.concatenate(blocks, axis=1)


def pick_columns(ref, code_of, depth, low, count):
    row = lax.broadcasted_iota(jnp.int32, (depth, 128), 0) + low
    row = row.astype(F32).astype(BF16)
    blocks = []
    for c in range(count):
        code = code_of(ref[pl.ds(c, 1), :]).astype(F32).astype(BF16)
        hit = jnp.broadcast_to(code, (depth, 128)) == row
        blocks.append(jnp.where(hit, jnp.ones_like(row), jnp.zeros_like(row)))
    return jnp.concatenate(blocks, axis=1)


def side_by_side(table, folds):
    depth = table.shape[0] // folds
    return jnp.concatenate([table[f * depth : (f + 1) * depth] for f in range(folds)], axis=1)


def choose(wide, which, folds):
    out = wide[:, :LATENT]
    for f in range(1, folds):
        out = jnp.where(which == f, wide[:, f * LATENT : (f + 1) * LATENT], out)
    return out


def centred_layer(second):
    exact = second.astype(F32)
    exact = exact - jnp.mean(exact, axis=-1, keepdims=True)
    high = exact.astype(BF16)
    low = (exact - high.astype(F32)).astype(BF16)
    return jnp.concatenate([high, low], axis=0)


def finish(pre, second):
    hidden = jnp.maximum(pre, 0.0).astype(BF16)
    centred = dot(jnp.concatenate([hidden, hidden], axis=1), second)
    spread = jnp.mean(centred * centred, axis=-1, keepdims=True)
    return centred * lax.rsqrt(spread + 1e-05)


def from_cells(table, index):
    code = jnp.where(index < CELLS, (index & 511) - 256, 512)
    wide = dot(pick_rows(code, 512, -256), table)
    return choose(wide, index >> 9, 4).astype(BF16)


def from_halo(table, index):
    code = jnp.where(index >= 0, index & 255, 512)
    wide = dot(pick_rows(code, 256, 0), table)
    return choose(wide, index >> 8, 4).astype(BF16)


def halo_table(flags, first, second, right, left, cross):
    a, b, c = first[...], second[...], cross[...]
    zero = jnp.zeros_like(a)
    up = jnp.where(flags[0] == 0, a, jnp.where(flags[0] == 1, b, jnp.where(flags[0] == 2, c, zero)))
    down = jnp.where(flags[1] == 0, a, jnp.where(flags[1] == 1, b, jnp.where(flags[1] == 2, c, zero)))
    west = jnp.where(flags[2] == 0, zero, left[...])
    east = jnp.where(flags[3] == 0, zero, right[...])
    return jnp.concatenate([up, down, west, east], axis=1)


def outgoing_kernel(nodes, rows, out):
    table = side_by_side(nodes[...], 4)
    out[...] = from_cells(table, column(rows, 0, 2) - 1)


def fine_local_kernel(nodes, edges, senders, receivers, first, out):
    table = side_by_side(nodes[...], 4)

    near = from_cells(table, jnp.concatenate([column(senders, 0, 8), column(receivers, 0, 8)], axis=0))
    out[...] = dot(jnp.concatenate([edges[...], near[:EDGES], near[EDGES:]], axis=1), first[...])


def edge_part(flags, pre, edges, senders, receivers, halo, edge_in, edge_out, new_edges, wide, sums):
    far = from_halo(halo_table(flags, *halo), column(senders, 0, 8) - CELLS)
    message = finish(pre[...] + dot(far, edge_in[LATENT : 2 * LATENT, :]), centred_layer(edge_out[...]))
    new_edges[...] = (edges[...].astype(F32) + message).astype(BF16)
    quarter = column(receivers, 0, 8) >> 9
    wide[...] = jnp.concatenate([jnp.where(quarter == f, message, 0.0) for f in range(4)], axis=1).astype(BF16)
    spread = pick_columns(receivers, lambda r: (r & 511) - 256, 512, -256, 8)
    total = dot(spread, wide[...]).astype(BF16)
    for f in range(4):
        sums[pl.ds(512 * f, 512), :] = total[:, f * LATENT : (f + 1) * LATENT]


def cell_part(at, nodes, sums, node_in, second):
    cells = nodes[at, :]
    inputs = jnp.concatenate([cells, sums[at, :]], axis=1)
    return (cells.astype(F32) + finish(dot(inputs, node_in[...]), second)).astype(BF16)


def fine_pool_kernel(
    flags, pre, edges, nodes, senders, receivers, first, second, right, left, cross,
    edge_in, edge_out, node_in, node_out, labels,
    new_nodes, new_edges, own, to_left, to_right, wide, sums, masked,
):
    halo = (first, second, right, left, cross)
    edge_part(flags, pre, edges, senders, receivers, halo, edge_in, edge_out, new_edges, wide, sums)
    layer = centred_layer(node_out[...])
    cells = cell_part(pl.ds(0, CELLS), nodes, sums, node_in, layer)
    new_nodes[...] = cells
    block = (column(labels, 0, 16) - flags[4]) >> 8
    masked[...] = jnp.concatenate(
        [jnp.where(block == b, cells.astype(F32), 0.0) for b in range(3)], axis=1
    ).astype(BF16)
    total = dot(pick_columns(labels, lambda r: r & 255, 256, 0, 16), masked[...])
    to_left[...] = total[:, :LATENT].astype(BF16)
    own[...] = total[:, LATENT : 2 * LATENT]
    to_right[...] = total[:, 2 * LATENT :].astype(BF16)


def fine_last_kernel(
    flags, pre, edges, nodes, senders, receivers, first, second, right, left, cross,
    edge_in, edge_out, node_in, node_out,
    new_nodes, new_edges, wide, sums, held_nodes, held_edges, sent,
):
    halo = (first, second, right, left, cross)
    edge_part(flags, pre, edges, senders, receivers, halo, edge_in, edge_out, held_edges, wide, sums)
    puts = [pltpu.make_async_copy(held_edges, new_edges, sent.at[0])]
    puts[0].start()
    layer = centred_layer(node_out[...])
    size = CELLS // CELL_PARTS
    for f in range(CELL_PARTS):
        at = pl.ds(f * size, size)
        held_nodes[at, :] = cell_part(at, nodes, sums, node_in, layer)
        puts.append(pltpu.make_async_copy(held_nodes.at[at, :], new_nodes.at[at, :], sent.at[1 + f]))
        puts[-1].start()
    for put in puts:
        put.wait()


def coarse_local_kernel(pooled, senders, receivers, first, out):
    index = jnp.concatenate([column(senders, 0, 8), column(receivers, 0, 8)], axis=0)
    near = dot(pick_rows(jnp.where(index < CLUS, index, 512), 256, 0), pooled[...]).astype(BF16)
    out[...] = dot(jnp.concatenate([near[:CEDGES], near[CEDGES:]], axis=1), first[...])


def coarse_kernel(
    flags, pre, pooled, senders, receivers, first, second, right, left, cross,
    edge_in, edge_out, node_in, node_out, out,
):
    table = halo_table(flags, first, second, right, left, cross)
    far = from_halo(table, column(senders, 0, 8) - CLUS)
    message = finish(pre[...] + dot(far, edge_in[:LATENT, :]), centred_layer(edge_out[...])).astype(BF16)
    gathered = dot(pick_columns(receivers, lambda r: r, 256, 0, 8), message).astype(BF16)
    own = pooled[...]
    inputs = jnp.concatenate([own, gathered], axis=1)
    out[...] = (own.astype(F32) + finish(dot(inputs, node_in[...]), centred_layer(node_out[...]))).astype(BF16)


def prolong_kernel(flags, cells, labels, own, left, right, rows, first, second, new_cells, outgoing):
    table = jnp.concatenate([left[...], own[...], right[...]], axis=1)
    index = column(labels, 0, 16) - flags[4]
    looked = choose(dot(pick_rows(index & 255, 256, 0), table), index >> 8, 3).astype(BF16)
    old = cells[...]
    update = finish(dot(jnp.concatenate([old, looked], axis=1), first[...]), centred_layer(second[...]))
    new = (old.astype(F32) + update).astype(BF16)
    new_cells[...] = new
    outgoing[...] = from_cells(side_by_side(new, 4), column(rows, 0, 2) - 1)


def shape(*dims, dtype=BF16):
    return jax.ShapeDtypeStruct(dims, dtype)


def call(kernel, outs, ins, args, name, estimate, scratch=(), where=None):
    return pl.pallas_call(
        kernel,
        out_shape=outs,
        in_specs=ins,
        out_specs=where or jax.tree.map(lambda _: VMEM, outs),
        scratch_shapes=scratch,
        compiler_params=PARAMS,
        cost_estimate=estimate,
        name=name,
    )(*args)


def snake(count_x, count_y):
    pairs = []
    for i in range(count_x):
        for j in range(count_y):
            if j % 2 == 0:
                to = (i + 1, j) if i % ROWS < ROWS - 1 else (i, j + 1)
            else:
                to = (i - 1, j) if i % ROWS > 0 else (i, j - 1)
            pairs.append((i * count_y + j, to[0] * count_y + to[1]))
    return pairs


def exchange(block):
    count_x, count_y = lax.axis_size("px"), lax.axis_size("py")
    ring = snake(count_x, count_y)
    crossing = []
    for k in range(ROWS - 1, count_x - 1, ROWS):
        crossing += [(k, k + 1), (k + 1, k)]
    left, right = exchange_row(block, block)
    first = lax.ppermute(block, ("px", "py"), ring)
    second = lax.ppermute(block, ("px", "py"), [(b, a) for a, b in ring])
    cross = lax.ppermute(block, "px", crossing)
    return first, second, right, left, cross


def exchange_row(to_left, to_right):
    count = lax.axis_size("py")
    from_left = lax.ppermute(to_right, "py", [(i, (i + 1) % count) for i in range(count)])
    from_right = lax.ppermute(to_left, "py", [((i + 1) % count, i) for i in range(count)])
    return from_left, from_right


def on_device(
    node_latents, edge_latents, edge_senders, edge_receivers, send_rows, clusters, coarse_senders, coarse_receivers,
    fine_edge_in, fine_edge_out, fine_node_in, fine_node_out,
    coarse_edge_in, coarse_edge_out, coarse_node_in, coarse_node_out, prolong_in, prolong_out,
):
    nodes, edges = node_latents[0, 0], edge_latents[0, 0]
    senders, receivers = edge_senders.reshape(8, 128), edge_receivers.reshape(8, 128)
    rows, labels = send_rows.reshape(2, 128) + 1, clusters.reshape(16, 128)
    csenders, creceivers = coarse_senders.reshape(8, 128), coarse_receivers.reshape(8, 128)
    i, j = lax.axis_index("px"), lax.axis_index("py")
    last_i, last_j = lax.axis_size("px") - 1, lax.axis_size("py") - 1
    core, along = j % 2, i % ROWS
    up = jnp.where(along > 0, core, jnp.where(i > 0, 2, 3))
    down = jnp.where(along < ROWS - 1, 1 - core, jnp.where(i < last_i, 2, 3))
    flags = jnp.stack([up, down, j > 0, j < last_j, (j - 1) * CLUS]).astype(jnp.int32)

    def fine_local(nodes, edges):
        return call(
            fine_local_kernel, shape(EDGES, LATENT, dtype=F32), [VMEM] * 5,
            (nodes, edges, senders, receivers, fine_edge_in), "fine_local", cost(4_000_000_000, 2_000_000),
        )

    weights = (fine_edge_in, fine_edge_out, fine_node_in, fine_node_out)
    scratch = [pltpu.VMEM((EDGES, 512), BF16), pltpu.VMEM((CELLS, LATENT), BF16)]

    outgoing = call(outgoing_kernel, shape(RIM, LATENT), [VMEM] * 2, (nodes, rows), "outgoing", cost(10**9, 10**6))
    halo = exchange(outgoing)
    pre = fine_local(nodes, edges)
    cells, edges_one, own, to_left, to_right = call(
        fine_pool_kernel,
        [shape(CELLS, LATENT), shape(EDGES, LATENT), shape(CLUS, LATENT, dtype=F32)] + [shape(CLUS, LATENT)] * 2,
        [SMEM] + [VMEM] * 15,
        (flags, pre, edges, nodes, senders, receivers, *halo, *weights, labels),
        "fine_pool", cost(4_000_000_000, 2_000_000), scratch + [pltpu.VMEM((CELLS, 384), BF16)],
    )
    from_left, from_right = exchange_row(to_left, to_right)
    pooled = ((own + from_left + from_right) / FAN).astype(BF16)
    halo = exchange(pooled)
    pre = call(
        coarse_local_kernel, shape(CEDGES, LATENT, dtype=F32), [VMEM] * 4,
        (pooled, csenders, creceivers, coarse_edge_in), "coarse_local", cost(10**9, 10**6),
    )
    coarse = call(
        coarse_kernel, shape(CLUS, LATENT), [SMEM] + [VMEM] * 13,
        (flags, pre, pooled, csenders, creceivers, *halo,
         coarse_edge_in, coarse_edge_out, coarse_node_in, coarse_node_out),
        "coarse", cost(2 * 10**9, 10**6),
    )
    left, right = exchange_row(coarse, coarse)
    cells_two, outgoing = call(
        prolong_kernel, [shape(CELLS, LATENT), shape(RIM, LATENT)], [SMEM] + [VMEM] * 8,
        (flags, cells, labels, coarse, left, right, rows, prolong_in, prolong_out),
        "prolong", cost(2 * 10**9, 10**6),
    )
    halo = exchange(outgoing)
    pre = fine_local(cells_two, edges_one)
    node_out, edge_out = call(
        fine_last_kernel, [shape(CELLS, LATENT), shape(EDGES, LATENT)], [SMEM] + [VMEM] * 14,
        (flags, pre, edges_one, cells_two, senders, receivers, *halo, *weights),
        "fine_last", cost(4_000_000_000, 2_000_000),
        scratch + [
            pltpu.VMEM((CELLS, LATENT), BF16), pltpu.VMEM((EDGES, LATENT), BF16),
            pltpu.SemaphoreType.DMA((1 + CELL_PARTS,)),
        ],
        [ANY, ANY],
    )
    return node_out[None, None], edge_out[None, None]


def solution(mesh):
    split = P("px", "py", None)
    cells = P("px", "py", None, None)
    return jax.shard_map(
        on_device,
        mesh=mesh,
        in_specs=(cells, cells) + (split,) * 6 + (P(),) * 10,
        out_specs=(cells, cells),
        check_vma=False,
    )
```

```python
import functools

import jax
import jax.numpy as jnp
from jax import lax
from jax.experimental import pallas as pl
from jax.experimental.pallas import tpu as pltpu
from jax.sharding import PartitionSpec as P

LATENT = 128
CELLS = 2048
EDGES = 1024
RIM = 256
CLUS = 256
CEDGES = 1024
FAN = 8
ROWS = 4
CELL_PARTS = 2
BF16 = jnp.bfloat16
F32 = jnp.float32
VMEM = pl.BlockSpec(memory_space=pltpu.VMEM)
ANY = pl.BlockSpec(memory_space=pl.ANY)
SMEM = pl.BlockSpec(memory_space=pltpu.SMEM)
PARAMS = pltpu.CompilerParams(vmem_limit_bytes=24 * 1024 * 1024)


def cost(flops, moved):
    return pl.CostEstimate(flops=flops, bytes_accessed=moved, transcendentals=0)


def dot(a, b):
    return jnp.dot(a, b, preferred_element_type=F32)


def column(ref, start, count):
    parts = []
    for k in range(count):
        row = ref[pl.ds(start + k, 1), :]
        parts.append(jnp.transpose(jnp.broadcast_to(row, (128, 128))))
    return jnp.concatenate(parts, axis=0)


def pick_rows(code, depth, low):
    code = code.astype(F32).astype(BF16)
    blocks = []
    for b in range(depth // 128):
        lane = lax.broadcasted_iota(jnp.int32, code.shape, 1) + (low + 128 * b)
        hit = code == lane.astype(F32).astype(BF16)
        blocks.append(jnp.where(hit, jnp.ones_like(code), jnp.zeros_like(code)))
    return jnp.concatenate(blocks, axis=1)


def pick_columns(ref, code_of, depth, low, count):
    row = lax.broadcasted_iota(jnp.int32, (depth, 128), 0) + low
    row = row.astype(F32).astype(BF16)
    blocks = []
    for c in range(count):
        code = code_of(ref[pl.ds(c, 1), :]).astype(F32).astype(BF16)
        hit = jnp.broadcast_to(code, (depth, 128)) == row
        blocks.append(jnp.where(hit, jnp.ones_like(row), jnp.zeros_like(row)))
    return jnp.concatenate(blocks, axis=1)


def side_by_side(table, folds):
    depth = table.shape[0] // folds
    return jnp.concatenate([table[f * depth : (f + 1) * depth] for f in range(folds)], axis=1)


def choose(wide, which, folds):
    out = wide[:, :LATENT]
    for f in range(1, folds):
        out = jnp.where(which == f, wide[:, f * LATENT : (f + 1) * LATENT], out)
    return out


def centred_layer(second):
    exact = second.astype(F32)
    exact = exact - jnp.mean(exact, axis=-1, keepdims=True)
    high = exact.astype(BF16)
    low = (exact - high.astype(F32)).astype(BF16)
    return jnp.concatenate([high, low], axis=0)


def finish(pre, second):
    hidden = jnp.maximum(pre, 0.0).astype(BF16)
    centred = dot(jnp.concatenate([hidden, hidden], axis=1), second)
    spread = jnp.mean(centred * centred, axis=-1, keepdims=True)
    return centred * lax.rsqrt(spread + 1e-05)


def from_cells(table, index):
    code = jnp.where(index < CELLS, (index & 511) - 256, 512)
    wide = dot(pick_rows(code, 512, -256), table)
    return choose(wide, index >> 9, 4).astype(BF16)


def from_halo(table, index):
    code = jnp.where(index >= 0, index & 255, 512)
    wide = dot(pick_rows(code, 256, 0), table)
    return choose(wide, index >> 8, 4).astype(BF16)


def halo_table(flags, first, second, right, left, cross):
    a, b, c = first[...], second[...], cross[...]
    zero = jnp.zeros_like(a)
    up = jnp.where(flags[0] == 0, a, jnp.where(flags[0] == 1, b, jnp.where(flags[0] == 2, c, zero)))
    down = jnp.where(flags[1] == 0, a, jnp.where(flags[1] == 1, b, jnp.where(flags[1] == 2, c, zero)))
    west = jnp.where(flags[2] == 0, zero, left[...])
    east = jnp.where(flags[3] == 0, zero, right[...])
    return jnp.concatenate([up, down, west, east], axis=1)


def outgoing_kernel(nodes, rows, out):
    table = side_by_side(nodes[...], 4)
    out[...] = from_cells(table, column(rows, 0, 2) - 1)


def local_product(table, edges, senders, receivers, first):
    near = from_cells(table, jnp.concatenate([column(senders, 0, 8), column(receivers, 0, 8)], axis=0))
    return dot(jnp.concatenate([edges[...], near[:EDGES], near[EDGES:]], axis=1), first[...])


def fine_local_kernel(nodes, edges, senders, receivers, first, out):
    out[...] = local_product(side_by_side(nodes[...], 4), edges, senders, receivers, first)


def edge_part(flags, pre, edges, senders, receivers, halo, edge_in, edge_out, new_edges, wide, sums):
    far = from_halo(halo_table(flags, *halo), column(senders, 0, 8) - CELLS)
    message = finish(pre[...] + dot(far, edge_in[LATENT : 2 * LATENT, :]), centred_layer(edge_out[...]))
    new_edges[...] = (edges[...].astype(F32) + message).astype(BF16)
    quarter = column(receivers, 0, 8) >> 9
    wide[...] = jnp.concatenate([jnp.where(quarter == f, message, 0.0) for f in range(4)], axis=1).astype(BF16)
    spread = pick_columns(receivers, lambda r: (r & 511) - 256, 512, -256, 8)
    total = dot(spread, wide[...]).astype(BF16)
    for f in range(4):
        sums[pl.ds(512 * f, 512), :] = total[:, f * LATENT : (f + 1) * LATENT]


def cell_part(at, nodes, sums, node_in, second):
    cells = nodes[at, :]
    inputs = jnp.concatenate([cells, sums[at, :]], axis=1)
    return (cells.astype(F32) + finish(dot(inputs, node_in[...]), second)).astype(BF16)


def fine_pool_kernel(
    flags, pre, edges, nodes, senders, receivers, first, second, right, left, cross,
    edge_in, edge_out, node_in, node_out, labels,
    new_nodes, new_edges, own, to_left, to_right, wide, sums, masked,
):
    halo = (first, second, right, left, cross)
    edge_part(flags, pre, edges, senders, receivers, halo, edge_in, edge_out, new_edges, wide, sums)
    layer = centred_layer(node_out[...])
    cells = cell_part(pl.ds(0, CELLS), nodes, sums, node_in, layer)
    new_nodes[...] = cells
    block = (column(labels, 0, 16) - flags[4]) >> 8
    masked[...] = jnp.concatenate(
        [jnp.where(block == b, cells.astype(F32), 0.0) for b in range(3)], axis=1
    ).astype(BF16)
    total = dot(pick_columns(labels, lambda r: r & 255, 256, 0, 16), masked[...])
    to_left[...] = total[:, :LATENT].astype(BF16)
    own[...] = total[:, LATENT : 2 * LATENT]
    to_right[...] = total[:, 2 * LATENT :].astype(BF16)


def fine_last_kernel(
    flags, pre, edges, nodes, senders, receivers, first, second, right, left, cross,
    edge_in, edge_out, node_in, node_out,
    new_nodes, new_edges, wide, sums, held_nodes, held_edges, sent,
):
    halo = (first, second, right, left, cross)
    edge_part(flags, pre, edges, senders, receivers, halo, edge_in, edge_out, held_edges, wide, sums)
    puts = [pltpu.make_async_copy(held_edges, new_edges, sent.at[0])]
    puts[0].start()
    layer = centred_layer(node_out[...])
    size = CELLS // CELL_PARTS
    for f in range(CELL_PARTS):
        at = pl.ds(f * size, size)
        held_nodes[at, :] = cell_part(at, nodes, sums, node_in, layer)
        puts.append(pltpu.make_async_copy(held_nodes.at[at, :], new_nodes.at[at, :], sent.at[1 + f]))
        puts[-1].start()
    for put in puts:
        put.wait()


def coarse_local_kernel(pooled, senders, receivers, first, out):
    index = jnp.concatenate([column(senders, 0, 8), column(receivers, 0, 8)], axis=0)
    near = dot(pick_rows(jnp.where(index < CLUS, index, 512), 256, 0), pooled[...]).astype(BF16)
    out[...] = dot(jnp.concatenate([near[:CEDGES], near[CEDGES:]], axis=1), first[...])


def coarse_kernel(
    flags, pre, pooled, senders, receivers, first, second, right, left, cross,
    edge_in, edge_out, node_in, node_out, out,
):
    table = halo_table(flags, first, second, right, left, cross)
    far = from_halo(table, column(senders, 0, 8) - CLUS)
    message = finish(pre[...] + dot(far, edge_in[:LATENT, :]), centred_layer(edge_out[...])).astype(BF16)
    gathered = dot(pick_columns(receivers, lambda r: r, 256, 0, 8), message).astype(BF16)
    own = pooled[...]
    inputs = jnp.concatenate([own, gathered], axis=1)
    out[...] = (own.astype(F32) + finish(dot(inputs, node_in[...]), centred_layer(node_out[...]))).astype(BF16)


def rim_kernel(flags, cells, labels, rows, rim, rim_labels):
    index = column(rows, 0, 2) - 1
    label = column(labels, 0, 16) - flags[4]
    rim[...] = from_cells(side_by_side(cells[...], 4), index)
    low = from_cells(side_by_side((label & 255).astype(F32).astype(BF16), 4), index)
    block = from_cells(side_by_side((label >> 8).astype(F32).astype(BF16), 4), index)
    rim_labels[...] = low.astype(F32).astype(jnp.int32) + 256 * block.astype(F32).astype(jnp.int32)


def lift(old, label, own, left, right, first, second):
    table = jnp.concatenate([left[...], own[...], right[...]], axis=1)
    looked = choose(dot(pick_rows(label & 255, 256, 0), table), label >> 8, 3).astype(BF16)
    update = finish(dot(jnp.concatenate([old, looked], axis=1), first[...]), centred_layer(second[...]))
    return (old.astype(F32) + update).astype(BF16)


def lift_rim_kernel(rim, rim_labels, own, left, right, first, second, out):
    out[...] = lift(rim[...], rim_labels[...], own, left, right, first, second)


def lift_local_kernel(
    flags, cells, labels, own, left, right, first, second, edges, senders, receivers, edge_in, new_cells, out
):
    label = column(labels, 0, 16) - flags[4]
    new = lift(cells[...], label, own, left, right, first, second)
    new_cells[...] = new
    out[...] = local_product(side_by_side(new, 4), edges, senders, receivers, edge_in)


def shape(*dims, dtype=BF16):
    return jax.ShapeDtypeStruct(dims, dtype)


def call(kernel, outs, ins, args, name, estimate, scratch=(), where=None):
    return pl.pallas_call(
        kernel,
        out_shape=outs,
        in_specs=ins,
        out_specs=where or jax.tree.map(lambda _: VMEM, outs),
        scratch_shapes=scratch,
        compiler_params=PARAMS,
        cost_estimate=estimate,
        name=name,
    )(*args)


def snake(count_x, count_y):
    pairs = []
    for i in range(count_x):
        for j in range(count_y):
            if j % 2 == 0:
                to = (i + 1, j) if i % ROWS < ROWS - 1 else (i, j + 1)
            else:
                to = (i - 1, j) if i % ROWS > 0 else (i, j - 1)
            pairs.append((i * count_y + j, to[0] * count_y + to[1]))
    return pairs


def exchange(block):
    count_x, count_y = lax.axis_size("px"), lax.axis_size("py")
    ring = snake(count_x, count_y)
    crossing = []
    for k in range(ROWS - 1, count_x - 1, ROWS):
        crossing += [(k, k + 1), (k + 1, k)]
    left, right = exchange_row(block, block)
    first = lax.ppermute(block, ("px", "py"), ring)
    second = lax.ppermute(block, ("px", "py"), [(b, a) for a, b in ring])
    cross = lax.ppermute(block, "px", crossing)
    return first, second, right, left, cross


def exchange_row(to_left, to_right):
    count = lax.axis_size("py")
    from_left = lax.ppermute(to_right, "py", [(i, (i + 1) % count) for i in range(count)])
    from_right = lax.ppermute(to_left, "py", [((i + 1) % count, i) for i in range(count)])
    return from_left, from_right


def on_device(
    node_latents, edge_latents, edge_senders, edge_receivers, send_rows, clusters, coarse_senders, coarse_receivers,
    fine_edge_in, fine_edge_out, fine_node_in, fine_node_out,
    coarse_edge_in, coarse_edge_out, coarse_node_in, coarse_node_out, prolong_in, prolong_out,
):
    nodes, edges = node_latents[0, 0], edge_latents[0, 0]
    senders, receivers = edge_senders.reshape(8, 128), edge_receivers.reshape(8, 128)
    rows, labels = send_rows.reshape(2, 128) + 1, clusters.reshape(16, 128)
    csenders, creceivers = coarse_senders.reshape(8, 128), coarse_receivers.reshape(8, 128)
    i, j = lax.axis_index("px"), lax.axis_index("py")
    last_i, last_j = lax.axis_size("px") - 1, lax.axis_size("py") - 1
    core, along = j % 2, i % ROWS
    up = jnp.where(along > 0, core, jnp.where(i > 0, 2, 3))
    down = jnp.where(along < ROWS - 1, 1 - core, jnp.where(i < last_i, 2, 3))
    flags = jnp.stack([up, down, j > 0, j < last_j, (j - 1) * CLUS]).astype(jnp.int32)

    weights = (fine_edge_in, fine_edge_out, fine_node_in, fine_node_out)
    scratch = [pltpu.VMEM((EDGES, 512), BF16), pltpu.VMEM((CELLS, LATENT), BF16)]

    outgoing = call(outgoing_kernel, shape(RIM, LATENT), [VMEM] * 2, (nodes, rows), "outgoing", cost(10**9, 10**6))
    halo = exchange(outgoing)
    pre = call(
        fine_local_kernel, shape(EDGES, LATENT, dtype=F32), [VMEM] * 5,
        (nodes, edges, senders, receivers, fine_edge_in), "fine_local", cost(4 * 10**9, 2 * 10**6),
    )
    cells, edges_one, own, to_left, to_right = call(
        fine_pool_kernel,
        [shape(CELLS, LATENT), shape(EDGES, LATENT), shape(CLUS, LATENT, dtype=F32)] + [shape(CLUS, LATENT)] * 2,
        [SMEM] + [VMEM] * 15,
        (flags, pre, edges, nodes, senders, receivers, *halo, *weights, labels),
        "fine_pool", cost(4_000_000_000, 2_000_000), scratch + [pltpu.VMEM((CELLS, 384), BF16)],
    )
    from_left, from_right = exchange_row(to_left, to_right)
    pooled = ((own + from_left + from_right) / FAN).astype(BF16)
    halo = exchange(pooled)
    pre = call(
        coarse_local_kernel, shape(CEDGES, LATENT, dtype=F32), [VMEM] * 4,
        (pooled, csenders, creceivers, coarse_edge_in), "coarse_local", cost(10**9, 10**6),
    )
    coarse = call(
        coarse_kernel, shape(CLUS, LATENT), [SMEM] + [VMEM] * 13,
        (flags, pre, pooled, csenders, creceivers, *halo,
         coarse_edge_in, coarse_edge_out, coarse_node_in, coarse_node_out),
        "coarse", cost(2 * 10**9, 10**6),
    )
    rim, rim_labels = call(
        rim_kernel, [shape(RIM, LATENT), shape(RIM, LATENT, dtype=jnp.int32)], [SMEM] + [VMEM] * 3,
        (flags, cells, labels, rows), "rim", cost(10**9, 10**6),
    )
    left, right = exchange_row(coarse, coarse)
    outgoing = call(
        lift_rim_kernel, shape(RIM, LATENT), [VMEM] * 7,
        (rim, rim_labels, coarse, left, right, prolong_in, prolong_out), "lift_rim", cost(10**8, 10**5),
    )
    halo = exchange(outgoing)
    cells_two, pre = call(
        lift_local_kernel, [shape(CELLS, LATENT), shape(EDGES, LATENT, dtype=F32)], [SMEM] + [VMEM] * 11,
        (flags, cells, labels, coarse, left, right, prolong_in, prolong_out,
         edges_one, senders, receivers, fine_edge_in),
        "lift_local", cost(4 * 10**9, 10**6),
    )
    node_out, edge_out = call(
        fine_last_kernel, [shape(CELLS, LATENT), shape(EDGES, LATENT)], [SMEM] + [VMEM] * 14,
        (flags, pre, edges_one, cells_two, senders, receivers, *halo, *weights),
        "fine_last", cost(4_000_000_000, 2_000_000),
        scratch + [
            pltpu.VMEM((CELLS, LATENT), BF16), pltpu.VMEM((EDGES, LATENT), BF16),
            pltpu.SemaphoreType.DMA((1 + CELL_PARTS,)),
        ],
        [ANY, ANY],
    )
    return node_out[None, None], edge_out[None, None]


def solution(mesh):
    split = P("px", "py", None)
    cells = P("px", "py", None, None)
    return jax.shard_map(
        on_device,
        mesh=mesh,
        in_specs=(cells, cells) + (split,) * 6 + (P(),) * 10,
        out_specs=(cells, cells),
        check_vma=False,
    )
```

```python
import functools

import jax
import jax.numpy as jnp
from jax import lax
from jax.experimental import pallas as pl
from jax.experimental.pallas import tpu as pltpu
from jax.sharding import PartitionSpec as P

LATENT = 128
CELLS = 2048
EDGES = 1024
RIM = 256
CLUS = 256
CEDGES = 1024
FAN = 8
ROWS = 4
CELL_PARTS = 2
BF16 = jnp.bfloat16
F32 = jnp.float32
VMEM = pl.BlockSpec(memory_space=pltpu.VMEM)
ANY = pl.BlockSpec(memory_space=pl.ANY)
SMEM = pl.BlockSpec(memory_space=pltpu.SMEM)
PARAMS = pltpu.CompilerParams(vmem_limit_bytes=24 * 1024 * 1024)


def cost(flops, moved):
    return pl.CostEstimate(flops=flops, bytes_accessed=moved, transcendentals=0)


def dot(a, b):
    return jnp.dot(a, b, preferred_element_type=F32)


def column(ref, start, count):
    parts = []
    for k in range(count):
        row = ref[pl.ds(start + k, 1), :]
        parts.append(jnp.transpose(jnp.broadcast_to(row, (128, 128))))
    return jnp.concatenate(parts, axis=0)


def pick_rows(code, depth, low):
    code = code.astype(F32).astype(BF16)
    blocks = []
    for b in range(depth // 128):
        lane = lax.broadcasted_iota(jnp.int32, code.shape, 1) + (low + 128 * b)
        hit = code == lane.astype(F32).astype(BF16)
        blocks.append(jnp.where(hit, jnp.ones_like(code), jnp.zeros_like(code)))
    return jnp.concatenate(blocks, axis=1)


def pick_columns(ref, code_of, depth, low, count):
    row = lax.broadcasted_iota(jnp.int32, (depth, 128), 0) + low
    row = row.astype(F32).astype(BF16)
    blocks = []
    for c in range(count):
        code = code_of(ref[pl.ds(c, 1), :]).astype(F32).astype(BF16)
        hit = jnp.broadcast_to(code, (depth, 128)) == row
        blocks.append(jnp.where(hit, jnp.ones_like(row), jnp.zeros_like(row)))
    return jnp.concatenate(blocks, axis=1)


def side_by_side(table, folds):
    depth = table.shape[0] // folds
    return jnp.concatenate([table[f * depth : (f + 1) * depth] for f in range(folds)], axis=1)


def choose(wide, which, folds):
    out = wide[:, :LATENT]
    for f in range(1, folds):
        out = jnp.where(which == f, wide[:, f * LATENT : (f + 1) * LATENT], out)
    return out


def centred_layer(second):
    exact = second.astype(F32)
    exact = exact - jnp.mean(exact, axis=-1, keepdims=True)
    high = exact.astype(BF16)
    low = (exact - high.astype(F32)).astype(BF16)
    return jnp.concatenate([high, low], axis=0)


def finish(pre, second):
    hidden = jnp.maximum(pre, 0.0).astype(BF16)
    centred = dot(jnp.concatenate([hidden, hidden], axis=1), second)
    spread = jnp.mean(centred * centred, axis=-1, keepdims=True)
    return centred * lax.rsqrt(spread + 1e-05)


def from_cells(table, index):
    code = jnp.where(index < CELLS, (index & 511) - 256, 512)
    wide = dot(pick_rows(code, 512, -256), table)
    return choose(wide, index >> 9, 4).astype(BF16)


def from_halo(table, index):
    code = jnp.where(index >= 0, index & 255, 512)
    wide = dot(pick_rows(code, 256, 0), table)
    return choose(wide, index >> 8, 4).astype(BF16)


def halo_table(flags, first, second, right, left, cross):
    a, b, c = first[...], second[...], cross[...]
    zero = jnp.zeros_like(a)
    up = jnp.where(flags[0] == 0, a, jnp.where(flags[0] == 1, b, jnp.where(flags[0] == 2, c, zero)))
    down = jnp.where(flags[1] == 0, a, jnp.where(flags[1] == 1, b, jnp.where(flags[1] == 2, c, zero)))
    west = jnp.where(flags[2] == 0, zero, left[...])
    east = jnp.where(flags[3] == 0, zero, right[...])
    return jnp.concatenate([up, down, west, east], axis=1)


def outgoing_kernel(nodes, rows, out):
    table = side_by_side(nodes[...], 4)
    out[...] = from_cells(table, column(rows, 0, 2) - 1)


def local_product(table, edges, senders, receivers, first):
    near = from_cells(table, jnp.concatenate([column(senders, 0, 8), column(receivers, 0, 8)], axis=0))
    return dot(jnp.concatenate([edges[...], near[:EDGES], near[EDGES:]], axis=1), first[...])


def fine_local_kernel(nodes, edges, senders, receivers, first, out):
    out[...] = local_product(side_by_side(nodes[...], 4), edges, senders, receivers, first)


def edge_part(flags, pre, edges, senders, receivers, halo, edge_in, edge_out, new_edges, wide, sums):
    far = from_halo(halo_table(flags, *halo), column(senders, 0, 8) - CELLS)
    message = finish(pre[...] + dot(far, edge_in[LATENT : 2 * LATENT, :]), centred_layer(edge_out[...]))
    new_edges[...] = (edges[...].astype(F32) + message).astype(BF16)
    quarter = column(receivers, 0, 8) >> 9
    wide[...] = jnp.concatenate([jnp.where(quarter == f, message, 0.0) for f in range(4)], axis=1).astype(BF16)
    spread = pick_columns(receivers, lambda r: (r & 511) - 256, 512, -256, 8)
    total = dot(spread, wide[...]).astype(BF16)
    for f in range(4):
        sums[pl.ds(512 * f, 512), :] = total[:, f * LATENT : (f + 1) * LATENT]


def cell_part(at, nodes, sums, node_in, second):
    cells = nodes[at, :]
    inputs = jnp.concatenate([cells, sums[at, :]], axis=1)
    return (cells.astype(F32) + finish(dot(inputs, node_in[...]), second)).astype(BF16)


def fine_pool_kernel(
    flags, pre, edges, nodes, senders, receivers, first, second, right, left, cross,
    edge_in, edge_out, node_in, node_out, labels,
    new_nodes, new_edges, own, to_left, to_right, wide, sums, masked,
):
    halo = (first, second, right, left, cross)
    edge_part(flags, pre, edges, senders, receivers, halo, edge_in, edge_out, new_edges, wide, sums)
    layer = centred_layer(node_out[...])
    cells = cell_part(pl.ds(0, CELLS), nodes, sums, node_in, layer)
    new_nodes[...] = cells
    block = (column(labels, 0, 16) - flags[4]) >> 8
    masked[...] = jnp.concatenate(
        [jnp.where(block == b, cells.astype(F32), 0.0) for b in range(3)], axis=1
    ).astype(BF16)
    total = dot(pick_columns(labels, lambda r: r & 255, 256, 0, 16), masked[...])
    to_left[...] = total[:, :LATENT].astype(BF16)
    own[...] = total[:, LATENT : 2 * LATENT]
    to_right[...] = total[:, 2 * LATENT :].astype(BF16)


def fine_last_kernel(
    flags, pre, edges, nodes, senders, receivers, first, second, cross, right, left,
    edge_in, edge_out, node_in, node_out,
    new_nodes, new_edges, wide, sums, held_nodes, held_edges, sent,
):
    halo = (first, second, right, left, cross)
    edge_part(flags, pre, edges, senders, receivers, halo, edge_in, edge_out, held_edges, wide, sums)
    puts = [pltpu.make_async_copy(held_edges, new_edges, sent.at[0])]
    puts[0].start()
    layer = centred_layer(node_out[...])
    size = CELLS // CELL_PARTS
    for f in range(CELL_PARTS):
        at = pl.ds(f * size, size)
        held_nodes[at, :] = cell_part(at, nodes, sums, node_in, layer)
        puts.append(pltpu.make_async_copy(held_nodes.at[at, :], new_nodes.at[at, :], sent.at[1 + f]))
        puts[-1].start()
    for put in puts:
        put.wait()


def coarse_local_kernel(pooled, senders, receivers, first, out):
    index = jnp.concatenate([column(senders, 0, 8), column(receivers, 0, 8)], axis=0)
    near = dot(pick_rows(jnp.where(index < CLUS, index, 512), 256, 0), pooled[...]).astype(BF16)
    out[...] = dot(jnp.concatenate([near[:CEDGES], near[CEDGES:]], axis=1), first[...])


def coarse_kernel(
    flags, pre, pooled, senders, receivers, first, second, right, left, cross,
    edge_in, edge_out, node_in, node_out, out,
):
    table = halo_table(flags, first, second, right, left, cross)
    far = from_halo(table, column(senders, 0, 8) - CLUS)
    message = finish(pre[...] + dot(far, edge_in[:LATENT, :]), centred_layer(edge_out[...])).astype(BF16)
    gathered = dot(pick_columns(receivers, lambda r: r, 256, 0, 8), message).astype(BF16)
    own = pooled[...]
    inputs = jnp.concatenate([own, gathered], axis=1)
    out[...] = (own.astype(F32) + finish(dot(inputs, node_in[...]), centred_layer(node_out[...]))).astype(BF16)


def rim_kernel(flags, cells, labels, rows, rim, rim_labels):
    index = column(rows, 0, 2) - 1
    label = column(labels, 0, 16) - flags[4]
    rim[...] = from_cells(side_by_side(cells[...], 4), index)
    low = from_cells(side_by_side((label & 255).astype(F32).astype(BF16), 4), index)
    block = from_cells(side_by_side((label >> 8).astype(F32).astype(BF16), 4), index)
    rim_labels[...] = low.astype(F32).astype(jnp.int32) + 256 * block.astype(F32).astype(jnp.int32)


def lift(old, label, own, left, right, first, second):
    table = jnp.concatenate([left[...], own[...], right[...]], axis=1)
    looked = choose(dot(pick_rows(label & 255, 256, 0), table), label >> 8, 3).astype(BF16)
    update = finish(dot(jnp.concatenate([old, looked], axis=1), first[...]), centred_layer(second[...]))
    return (old.astype(F32) + update).astype(BF16)


def lift_rim_kernel(rim, rim_labels, own, left, right, first, second, out):
    out[...] = lift(rim[...], rim_labels[...], own, left, right, first, second)


def lift_local_kernel(
    flags, cells, labels, own, left, right, first, second, edges, senders, receivers, edge_in, new_cells, out
):
    label = column(labels, 0, 16) - flags[4]
    new = lift(cells[...], label, own, left, right, first, second)
    new_cells[...] = new
    out[...] = local_product(side_by_side(new, 4), edges, senders, receivers, edge_in)


def shape(*dims, dtype=BF16):
    return jax.ShapeDtypeStruct(dims, dtype)


def call(kernel, outs, ins, args, name, estimate, scratch=(), where=None):
    return pl.pallas_call(
        kernel,
        out_shape=outs,
        in_specs=ins,
        out_specs=where or jax.tree.map(lambda _: VMEM, outs),
        scratch_shapes=scratch,
        compiler_params=PARAMS,
        cost_estimate=estimate,
        name=name,
    )(*args)


def snake(count_x, count_y):
    pairs = []
    for i in range(count_x):
        for j in range(count_y):
            if j % 2 == 0:
                to = (i + 1, j) if i % ROWS < ROWS - 1 else (i, j + 1)
            else:
                to = (i - 1, j) if i % ROWS > 0 else (i, j - 1)
            pairs.append((i * count_y + j, to[0] * count_y + to[1]))
    return pairs


def exchange(block):
    count_x, count_y = lax.axis_size("px"), lax.axis_size("py")
    ring = snake(count_x, count_y)
    crossing = []
    for k in range(ROWS - 1, count_x - 1, ROWS):
        crossing += [(k, k + 1), (k + 1, k)]
    left, right = exchange_row(block, block)
    first = lax.ppermute(block, ("px", "py"), ring)
    second = lax.ppermute(block, ("px", "py"), [(b, a) for a, b in ring])
    cross = lax.ppermute(block, "px", crossing)
    return first, second, right, left, cross


def exchange_row(to_left, to_right):
    count = lax.axis_size("py")
    from_left = lax.ppermute(to_right, "py", [(i, (i + 1) % count) for i in range(count)])
    from_right = lax.ppermute(to_left, "py", [((i + 1) % count, i) for i in range(count)])
    return from_left, from_right


def on_device(
    node_latents, edge_latents, edge_senders, edge_receivers, send_rows, clusters, coarse_senders, coarse_receivers,
    fine_edge_in, fine_edge_out, fine_node_in, fine_node_out,
    coarse_edge_in, coarse_edge_out, coarse_node_in, coarse_node_out, prolong_in, prolong_out,
):
    nodes, edges = node_latents[0, 0], edge_latents[0, 0]
    senders, receivers = edge_senders.reshape(8, 128), edge_receivers.reshape(8, 128)
    rows, labels = send_rows.reshape(2, 128) + 1, clusters.reshape(16, 128)
    csenders, creceivers = coarse_senders.reshape(8, 128), coarse_receivers.reshape(8, 128)
    i, j = lax.axis_index("px"), lax.axis_index("py")
    last_i, last_j = lax.axis_size("px") - 1, lax.axis_size("py") - 1
    core, along = j % 2, i % ROWS
    up = jnp.where(along > 0, core, jnp.where(i > 0, 2, 3))
    down = jnp.where(along < ROWS - 1, 1 - core, jnp.where(i < last_i, 2, 3))
    flags = jnp.stack([up, down, j > 0, j < last_j, (j - 1) * CLUS]).astype(jnp.int32)

    weights = (fine_edge_in, fine_edge_out, fine_node_in, fine_node_out)
    scratch = [pltpu.VMEM((EDGES, 512), BF16), pltpu.VMEM((CELLS, LATENT), BF16)]

    outgoing = call(outgoing_kernel, shape(RIM, LATENT), [VMEM] * 2, (nodes, rows), "outgoing", cost(10**9, 10**6))
    halo = exchange(outgoing)
    pre = call(
        fine_local_kernel, shape(EDGES, LATENT, dtype=F32), [VMEM] * 5,
        (nodes, edges, senders, receivers, fine_edge_in), "fine_local", cost(4 * 10**9, 2 * 10**6),
    )
    cells, edges_one, own, to_left, to_right = call(
        fine_pool_kernel,
        [shape(CELLS, LATENT), shape(EDGES, LATENT), shape(CLUS, LATENT, dtype=F32)] + [shape(CLUS, LATENT)] * 2,
        [SMEM] + [VMEM] * 15,
        (flags, pre, edges, nodes, senders, receivers, *halo, *weights, labels),
        "fine_pool", cost(4_000_000_000, 2_000_000), scratch + [pltpu.VMEM((CELLS, 384), BF16)],
    )
    from_left, from_right = exchange_row(to_left, to_right)
    pooled = ((own + from_left + from_right) / FAN).astype(BF16)
    halo = exchange(pooled)
    pre = call(
        coarse_local_kernel, shape(CEDGES, LATENT, dtype=F32), [VMEM] * 4,
        (pooled, csenders, creceivers, coarse_edge_in), "coarse_local", cost(10**9, 10**6),
    )
    coarse = call(
        coarse_kernel, shape(CLUS, LATENT), [SMEM] + [VMEM] * 13,
        (flags, pre, pooled, csenders, creceivers, *halo,
         coarse_edge_in, coarse_edge_out, coarse_node_in, coarse_node_out),
        "coarse", cost(2 * 10**9, 10**6),
    )
    rim, rim_labels = call(
        rim_kernel, [shape(RIM, LATENT), shape(RIM, LATENT, dtype=jnp.int32)], [SMEM] + [VMEM] * 3,
        (flags, cells, labels, rows), "rim", cost(10**9, 10**6),
    )
    left, right = exchange_row(coarse, coarse)
    outgoing = call(
        lift_rim_kernel, shape(RIM, LATENT), [VMEM] * 7,
        (rim, rim_labels, coarse, left, right, prolong_in, prolong_out), "lift_rim", cost(10**8, 10**5),
    )
    halo = exchange(outgoing)
    cells_two, pre = call(
        lift_local_kernel, [shape(CELLS, LATENT), shape(EDGES, LATENT, dtype=F32)], [SMEM] + [VMEM] * 11,
        (flags, cells, labels, coarse, left, right, prolong_in, prolong_out,
         edges_one, senders, receivers, fine_edge_in),
        "lift_local", cost(4 * 10**9, 10**6),
    )
    node_out, edge_out = call(
        fine_last_kernel, [shape(CELLS, LATENT), shape(EDGES, LATENT)], [SMEM] + [VMEM] * 14,
        (flags, pre, edges_one, cells_two, senders, receivers, *[halo[k] for k in (0, 1, 4, 2, 3)], *weights),
        "fine_last", cost(4_000_000_000, 2_000_000),
        scratch + [
            pltpu.VMEM((CELLS, LATENT), BF16), pltpu.VMEM((EDGES, LATENT), BF16),
            pltpu.SemaphoreType.DMA((1 + CELL_PARTS,)),
        ],
        [ANY, ANY],
    )
    return node_out[None, None], edge_out[None, None]


def solution(mesh):
    split = P("px", "py", None)
    cells = P("px", "py", None, None)
    return jax.shard_map(
        on_device,
        mesh=mesh,
        in_specs=(cells, cells) + (split,) * 6 + (P(),) * 10,
        out_specs=(cells, cells),
        check_vma=False,
    )
```
